256 devices in a mesh: dp: 16 (over x, y), tensor: 16 (over z, core).
Axes of the slice: x: 4, y: 4, z: 8, core: 2. Of those that a mesh axis runs over, the one named last changes fastest.
Arguments:
- hidden: bfloat16 [2048, 16384], P('dp', 'tensor'), may hold values from -6 to 6
- branch: bfloat16 [2048, 16384], P('dp', 'tensor'), may hold values from -6 to 6
- gain: float32 [16384], P('tensor'), may hold values from 0.25 to 1.75
- damping: float32 [16384], P('tensor'), may hold values from 0.5 to 2
Outputs:
- schur: float32 [16384, 16384], P('dp', 'tensor')
- first_panel: float32 [16384, 512], P('dp')
- second_panel: float32 [16384, 512], P('dp')
The draws below stay inside these ranges and needn't reach their ends.
All inputs are finite; a program needn't handle non-finite values.
Results may differ from the reference program's by a relative error of at most 0.0034.
Values may be sent and summed in bfloat16 or wider, within the bound.
A program may use at most 128 MiB of HBM per device.

```python
import math
import jax
import jax.numpy as jnp
from jax import lax

D = 16384
PANEL = 512
TOKENS = 2048


def levels(stream_key, shape, split, least, top_value):
    factor_of, own = 1.0, jax.random.fold_in(stream_key, 6)
    for dim, shards_of in split:
        heights = jnp.exp(jax.random.uniform(jax.random.fold_in(own, dim), (shards_of,), jnp.float32, least / len(split), top_value / len(split)))
        factor_of = factor_of * jnp.repeat(heights, shape[dim] // shards_of).reshape([-1 if axis == dim else 1 for axis in range(len(shape))])
    return factor_of


def noise(rng, dims, deviation, limit, shards=(), kind=jnp.bfloat16):
    factor_of = levels(rng, dims, shards, -0.22, 0.18) if shards else 1.0
    values = jax.random.normal(rng, dims, jnp.float32) * deviation * factor_of
    return jnp.minimum(jnp.maximum(values, -limit), limit).astype(kind)


def setup_inputs(seed: int = 0) -> dict:
    key_list = jax.random.split(jax.random.key(seed), 5)
    hidden = noise(key_list[0], (TOKENS, D), 1.0, 6.0, ((0, 16), (1, 16)))
    branch = noise(key_list[1], (TOKENS, D), 0.7, 6.0, ((0, 16), (1, 16)))
    gain = jnp.clip(1.0 + 0.15 * jax.random.normal(key_list[2], (D,), jnp.float32), 0.25, 1.75)
    damping = jnp.clip(jnp.exp(math.log(2.0) - 1.3862944 * jax.random.uniform(key_list[3], (D,), jnp.float32) ** levels(key_list[3], (D,), ((0, 16),), -0.2, 0.2)), 0.5, 2.0)
    return dict(hidden=hidden, branch=branch, gain=gain, damping=damping)


def reference(hidden, branch, gain, damping):
    summed = hidden.astype(jnp.float32) + branch.astype(jnp.float32)
    meansq = lax.optimization_barrier(jnp.mean(summed * summed, axis=1, keepdims=True))
    normed = (summed * lax.rsqrt(meansq + 1e-05) * gain[None, :]).astype(jnp.bfloat16)
    gram = lax.dot_general(normed.astype(jnp.float32), normed.astype(jnp.float32), (((0,), (0,)), ((), ())), preferred_element_type=jnp.float32)
    eye_full = jnp.arange(D)[:, None] == jnp.arange(D)[None, :]
    state = gram / TOKENS + jnp.where(eye_full, damping[None, :], jnp.zeros((), jnp.float32))
    panels = []
    for step in range(2):
        offset = step * PANEL
        pivot = state[offset:offset + PANEL, offset:offset + PANEL]
        factor = jnp.linalg.cholesky(pivot)
        inverse = lax.linalg.triangular_solve(factor, jnp.eye(PANEL, dtype=factor.dtype), left_side=True, lower=True)
        panel = lax.dot_general(state[:, offset:offset + PANEL], inverse, (((1,), (1,)), ((), ())), precision=lax.Precision.HIGHEST)
        state = state - lax.dot_general(panel, panel, (((1,), (1,)), ((), ())), precision=lax.Precision.HIGHEST)
        panels.append(panel)
    return (state, panels[0], panels[1])
```

```python
import functools

import jax
import jax.numpy as jnp
from jax import lax
from jax.experimental import pallas as pl
from jax.experimental.pallas import tpu as pltpu
from jax.sharding import PartitionSpec as P

D = 16384
TOKENS = 2048
LEAD = 1024
MESH = pl.DeviceIdType.MESH
f32, bf16 = jnp.float32, jnp.bfloat16
NN = (((1,), (0,)), ((), ()))
NT = (((1,), (1,)), ((), ()))
TN = (((0,), (0,)), ((), ()))


def split(x):
    high = x.astype(bf16)
    return high, (x - high.astype(f32)).astype(bf16)


def dot1(x, y, dims):
    return lax.dot_general(x, y, dims, preferred_element_type=f32)


def dot3(x, y, dims):
    (xh, xl), (yh, yl) = split(x), split(y)
    return dot1(xh, yh, dims) + (dot1(xh, yl, dims) + dot1(xl, yh, dims))


def iota(shape, dim):
    return lax.broadcasted_iota(jnp.int32, shape, dim)


def base_inverse(T, b=32, n=128):
    sub, lane = iota((b, n), 0), iota((b, n), 1)
    for o in range(0, n, b):
        R = T[o : o + b, :]
        C = [jnp.broadcast_to(R[:, o + j : o + j + 1], (b, n)) for j in range(b)]
        R = jnp.where((lane >= o) & (lane < o + b), (lane - o == sub).astype(f32), R)
        for j in range(b):
            r = lax.rsqrt(C[j][j : j + 1, :])
            column = jnp.where(sub > j, C[j] * r, 0.0)
            row = R[j : j + 1, :] * r
            R = jnp.where(sub == j, row, R - column * row)
            for m in range(j + 1, b):
                C[m] = C[m] - column * column[m : m + 1, :]
        T[o : o + b, :] = R
        lo = o + b
        if lo < n:
            (Uh, Ul), (Rh, Rl) = split(jnp.where(lane >= lo, R, 0.0)), split(R)
            update = dot1(
                jnp.concatenate([Uh, Uh, Ul], 0), jnp.concatenate([Rh, Rl, Rh], 0), TN
            )
            ln = iota((n - lo, n), 1)
            T[lo:, :] = jnp.where((ln >= o) & (ln < lo), 0.0, T[lo:, :]) - update[lo:, :]
    T[...] = jnp.where(iota((n, n), 0) >= iota((n, n), 1), T[...], 0.0)


def factor(T, block):
    n = LEAD // 128
    for k in range(n):
        rows = slice(k * 128, k * 128 + 128)
        block[...] = T[rows, rows]
        base_inverse(block)
        inverse = block[...]
        if k:
            T[rows, : k * 128] = dot3(inverse, T[rows, : k * 128], NN)
        T[rows, rows] = inverse
        if k < n - 1:
            right = slice(k * 128 + 128, LEAD)
            U = dot3(inverse, T[rows, right], NN)
            T[rows, right] = U
            Uh, Ul = split(U)
            left = T[rows, : k * 128 + 128]
            Lh, Ll = split(left)
            for i in range(k + 1, n):
                at = slice((i - k - 1) * 128, (i - k) * 128)
                own = slice(i * 128, i * 128 + 128)
                uh, ul = Uh[:, at].T, Ul[:, at].T
                low = dot1(uh, Lh, NN) + (dot1(uh, Ll, NN) + dot1(ul, Lh, NN))
                if k:
                    T[own, : k * 128] = T[own, : k * 128] - low[:, : k * 128]
                T[own, rows] = -low[:, k * 128 :]
                rest = slice((i - k - 1) * 128, None)
                T[own, i * 128 :] = T[own, i * 128 :] - (
                    dot1(uh, Uh[:, rest], NN)
                    + (dot1(uh, Ul[:, rest], NN) + dot1(ul, Uh[:, rest], NN))
                )


def compute_body(
    A, B, N0, lead_damping, own_damping, tile, first, second, T, block, lead_t, rows_t, panel, moved_t
):
    on_diagonal = lax.axis_index("dp") == lax.axis_index("tensor")
    step = 256

    def turn(i, _):
        at = pl.ds(pl.multiple_of(i * 128, 128), 128)
        for h in range(2):
            rows = slice(h * 512, h * 512 + 512)
            lead_t[rows, at] = N0[h, at, :].T
            rows_t[rows, at] = B[h, at, :].T
        return 0

    lax.fori_loop(0, TOKENS // 128, turn, 0)

    def lead_gram(i, _):
        at = pl.ds(pl.multiple_of(i * 128, 128), 128)
        lhs = lead_t[at, :]
        for h in range(2):
            T[at, h * 512 : h * 512 + 512] = dot1(lhs, N0[h], NN) * (1.0 / TOKENS)
        return 0

    lax.fori_loop(0, LEAD // 128, lead_gram, 0)
    eye = iota((128, 128), 0) == iota((128, 128), 1)
    for k in range(LEAD // 128):
        at = slice(k * 128, k * 128 + 128)
        T[at, at] = T[at, at] + jnp.where(eye, lead_damping[k : k + 1, :], 0.0)
    factor(T, block)
    n = LEAD // 128
    for k in range(n - 1):
        T[k * 128 : k * 128 + 128, k * 128 + 128 :] = jnp.zeros((128, LEAD - 128 - k * 128), f32)

    dp, tensor = lax.axis_index("dp"), lax.axis_index("tensor")
    for q in range(LEAD // step):
        cols = slice(q * step, q * step + step)
        wide = (q + 1) * step
        weight_h, weight_l = split(T[cols, :wide])

        def own_rows(i, _):
            at = pl.ds(pl.multiple_of(i * step, step), step)
            if q == 0:
                lhs = rows_t[at, :]
                for h in range(2):
                    panel[at, h * 512 : h * 512 + 512] = dot1(lhs, N0[h], NN) * (1.0 / TOKENS)
                rr, cc = iota((step, LEAD), 0), iota((step, LEAD), 1)
                damp = jnp.concatenate([lead_damping[j : j + 1, :] for j in range(8)], 1)
                here = (rr + i * step == cc) & (dp == 0)
                panel[at, :] = panel[at, :] + jnp.where(here, damp, 0.0)
            out = first if q < 2 else second
            sh, sl = split(panel[at, :wide])
            out[at, (q % 2) * step : (q % 2) * step + step] = dot1(sh, weight_h, NT) + (
                dot1(sh, weight_l, NT) + dot1(sl, weight_h, NT)
            )
            return 0

        lax.fori_loop(0, LEAD // step, own_rows, 0)

        def own_cols(i, _):
            at = pl.ds(pl.multiple_of(i * step, step), step)
            if q == 0:
                rhs = A[:, at]
                moved_t[:, at] = dot1(lead_t[...], rhs, NN) * (1.0 / TOKENS)
                damp = jnp.concatenate([lead_damping[j : j + 1, :] for j in range(8)], 1)
                rr, cc = iota((LEAD, step), 0), iota((LEAD, step), 1)
                diag = jnp.concatenate(
                    [
                        jnp.broadcast_to(damp[:, j * 128 : j * 128 + 128].T, (128, step))
                        for j in range(8)
                    ],
                    0,
                )
                here = (cc + i * step == rr) & (tensor == 0)
                moved_t[:, at] = moved_t[:, at] + jnp.where(here, diag, 0.0)
            return 0

        if q == 0:
            lax.fori_loop(0, LEAD // step, own_cols, 0)

    def finish(i, _):
        at = pl.ds(pl.multiple_of(i * step, step), step)
        sh, sl = split(moved_t[:, at])
        parts = []
        for q in range(LEAD // step):
            wide = (q + 1) * step
            wh, wl = split(T[q * step : wide, :wide])
            parts.append(
                dot1(wh, sh[:wide], NN) + (dot1(wh, sl[:wide], NN) + dot1(wl, sh[:wide], NN))
            )
        moved = jnp.concatenate(parts, 0)
        mh, ml = split(moved)
        gram = dot1(rows_t[...], A[:, at], NN) * (1.0 / TOKENS)
        ph, plo = split(first[...])
        qh, qlo = split(second[...])
        half = LEAD // 2
        gram = gram - (dot1(ph, mh[:half], NN) + dot1(qh, mh[half:], NN))
        gram = gram - (dot1(ph, ml[:half], NN) + dot1(qh, ml[half:], NN))
        gram = gram - (dot1(plo, mh[:half], NN) + dot1(qlo, mh[half:], NN))
        tile[:, at] = gram
        return 0

    lax.fori_loop(0, LEAD // step, finish, 0)

    @pl.when(on_diagonal)
    def _():
        for k in range(n):
            at = slice(k * 128, k * 128 + 128)
            tile[at, at] = tile[at, at] + jnp.where(eye, own_damping[k : k + 1, :], 0.0)


def compute(A, B, N0, lead_damping, own_damping):
    vm = pl.BlockSpec(memory_space=pltpu.VMEM)
    return pl.pallas_call(
        compute_body,
        out_shape=(
            jax.ShapeDtypeStruct((LEAD, LEAD), f32),
            jax.ShapeDtypeStruct((LEAD, LEAD // 2), f32),
            jax.ShapeDtypeStruct((LEAD, LEAD // 2), f32),
        ),
        in_specs=[vm] * 5,
        out_specs=(vm,) * 3,
        scratch_shapes=[
            pltpu.VMEM((LEAD, LEAD), f32),
            pltpu.VMEM((128, 128), f32),
            pltpu.VMEM((LEAD, TOKENS), bf16),
            pltpu.VMEM((LEAD, TOKENS), bf16),
            pltpu.VMEM((LEAD, LEAD), f32),
            pltpu.VMEM((LEAD, LEAD), f32),
        ],
        compiler_params=pltpu.CompilerParams(vmem_limit_bytes=60 * 2**20),
    )(A, B, N0, lead_damping, own_damping)


def strip_of(kind, k, x, y):
    if kind == 0:
        return (slice(None), lax.rem(y + k, 4), pl.ds(0, 64))
    return (lax.rem(x + k, 4), slice(None), pl.ds(64, 64))


def gather_body(
    hidden, branch, gain, damping, A, B, N0, lead_damping,
    parts, n_sem, part_send, part_recv, z_send, z_recv, sib_send, sib_recv,
    g_send, g_recv, x_send, x_recv, b_send, b_recv, e_send, e_recv, local_sem,
):
    d, t = lax.axis_index("dp"), lax.axis_index("tensor")
    x, y, z, c = d // 4, d % 4, t // 2, t % 2
    sibling = (d, t + 1 - 2 * c)
    along = {
        (0, 1): (lax.rem(x + 1, 4) * 4 + y, t),
        (0, -1): (lax.rem(x + 3, 4) * 4 + y, t),
        (1, 1): (x * 4 + lax.rem(y + 1, 4), t),
        (1, -1): (x * 4 + lax.rem(y + 3, 4), t),
    }
    up = (d, lax.rem(z + 1, 8) * 2 + c)
    down = (d, lax.rem(z + 7, 8) * 2 + c)
    same = [(d, lax.rem(t + i, 16)) for i in range(1, 16)]

    barrier = pltpu.get_barrier_semaphore()
    partners = same + list(along.values())
    for partner in partners:
        pl.semaphore_signal(barrier, inc=1, device_id=partner, device_id_type=MESH)

    def remote(src, dst, send, recv, to):
        return pltpu.make_async_remote_copy(
            src_ref=src, dst_ref=dst, send_sem=send, recv_sem=recv, device_id=to, device_id_type=MESH
        )

    total = hidden[...].astype(f32) + branch[...].astype(f32)
    own = jnp.broadcast_to(jnp.sum(total * total, axis=1, keepdims=True), (128, 128))
    parts[0, 0:8, :] = own.T[0:8, :]
    parts[0, 8:16, :] = damping[...]
    pl.semaphore_wait(barrier, len(partners))
    part_copies = [
        remote(parts.at[0], parts.at[i], part_send.at[i], part_recv.at[i], same[i - 1])
        for i in range(1, 16)
    ]
    for copy in part_copies:
        copy.start()
    for copy in part_copies:
        copy.wait_recv()
    squares = parts[0, 0:1, :]
    for i in range(1, 16):
        squares = squares + parts[i, 0:1, :]
    lead_damping[...] = parts[t, 8:16, :]
    scale = lax.rsqrt(squares / D + 1e-05)
    column = jnp.broadcast_to(scale, (128, 128)).T
    for j in range(8):
        at = slice(j * 128, j * 128 + 128)
        block = hidden[:, at].astype(f32) + branch[:, at].astype(f32)
        A[x, y, :, at] = (block * column * gain[j : j + 1, :]).astype(bf16)

    def both_ways(ref, which):
        copies = {}
        for kind in range(2):
            at = (x, y, pl.ds(64 * kind, 64))
            for side, s in ((1, 0), (-1, 1)):
                copies[kind, side] = remote(
                    ref.at[at], ref.at[at], g_send.at[which, 0, kind, s], g_recv.at[which, 0, kind, s],
                    along[kind, side],
                )
        return copies

    def pass_on(ref, which):
        copies = {}
        for kind in range(2):
            for side, s in ((1, 0), (-1, 1)):
                back = 4 - side
                at = (lax.rem(x + back, 4), y) if kind == 0 else (x, lax.rem(y + back, 4))
                at = at + (pl.ds(64 * kind + 32 * s, 32),)
                copies[kind, side] = remote(
                    ref.at[at], ref.at[at], g_send.at[which, 1, kind, s], g_recv.at[which, 1, kind, s],
                    along[kind, side],
                )
        return copies

    def strips(ref, which):
        copies = {}
        for kind in range(2):
            at = strip_of(kind, 0, x, y)
            for side, s in ((1, 0), (-1, 1)):
                copies[kind, side] = remote(
                    ref.at[at], ref.at[at], g_send.at[which, 2, kind, s], g_recv.at[which, 2, kind, s],
                    along[1 - kind, side],
                )
        return copies

    def strips_on(ref, which):
        copies = {}
        for kind in range(2):
            for side, s in ((1, 0), (-1, 1)):
                at = strip_of(kind, 4 - side, x, y)
                at = at[:2] + (pl.ds(64 * kind + 32 * s, 32),)
                copies[kind, side] = remote(
                    ref.at[at], ref.at[at], g_send.at[which, 3, kind, s], g_recv.at[which, 3, kind, s],
                    along[1 - kind, side],
                )
        return copies

    def start(copies):
        for copy in copies.values():
            copy.start()
        return copies

    def arrive(copies):
        for copy in copies.values():
            copy.wait_recv()

    def sent(copies):
        for copy in copies.values():
            copy.wait_send()

    a_first = start(both_ways(A, 0))

    half = N0.at[c]
    chunks = [pl.ds(32 * q, 32) for q in range(4)]
    source = (x, y)

    @pl.when(t == 0)
    def _():
        for q in range(4):
            remote(
                A.at[x, y, chunks[q], pl.ds(512, 512)], N0.at[1, x, y, chunks[q]],
                sib_send.at[q], z_recv.at[q], sibling,
            ).start()
        N0[0, x, y] = A[x, y, :, 0:512]

    rising, falling = [], []
    for q in range(4):
        at = half.at[source + (chunks[q],)]
        rising.append(remote(at, at, z_send.at[0, q], z_recv.at[q], up))
        falling.append(remote(at, at, z_send.at[1, q], z_recv.at[q], down))

        @pl.when(t != 0)
        def _():
            rising[q].wait_recv()

        @pl.when(z < 4)
        def _():
            rising[q].start()

        @pl.when((z == 0) | (z > 5))
        def _():
            falling[q].start()

    n_first = start(both_ways(half, 1))
    arrive(a_first)
    a_second = start(pass_on(A, 0))
    arrive(n_first)
    n_second = start(pass_on(half, 1))

    def give(kind, k):
        at = (c,) + strip_of(kind, k, x, y)
        copy = remote(N0.at[at], N0.at[at], x_send.at[kind, k], x_recv.at[kind, k], sibling)
        copy.start()
        return copy

    gifts = []
    arrive(n_second)
    n_third = start(strips(half, 1))
    gifts += [give(kind, 0) for kind in range(2)]
    arrive(a_second)
    a_third = start(strips(A, 0))

    origin = d // 2
    rise = lax.rem(z - origin + 8, 8)
    at_origin = rise == 0
    is_source = t == d

    def piece(kind, k, j):
        if kind == 0:
            return (j, lax.rem(y + k, 4), pl.ds(0, 64))
        return (lax.rem(x + k, 4), j, pl.ds(64, 64))

    order = {0: 0, 1: 1, 3: 2, 2: 3}

    def b_from_source(k):
        @pl.when(is_source)
        def _():
            for kind in range(2):
                at = strip_of(kind, k, x, y)
                n = order[k]
                for j in range(4):
                    sub = piece(kind, k, j)
                    remote(
                        A.at[sub + (pl.ds(pl.multiple_of(c * 512, 512), 512),)], B.at[(c,) + sub],
                        b_send.at[kind, n, j], b_recv.at[kind, n, j], up if kind == 0 else down,
                    ).start()
                    remote(
                        A.at[sub + (pl.ds(pl.multiple_of(512 - c * 512, 512), 512),)], B.at[(1 - c,) + sub],
                        e_send.at[kind, n, 1 + j], b_recv.at[kind, n, j], sibling,
                    ).start()
                remote(
                    A.at[at + (pl.ds(pl.multiple_of(c * 512, 512), 512),)], B.at[(c,) + at],
                    e_send.at[kind, n, 0], e_recv.at[kind, n], sibling,
                ).start()
                for h in range(2):
                    pltpu.make_async_copy(
                        A.at[at + (pl.ds(512 * h, 512),)], B.at[(h,) + at], local_sem.at[kind, n, h]
                    ).start()

    def b_relay(k):
        n = order[k]
        for j in range(4):
            for kind in range(2):
                sub = (c,) + piece(kind, k, j)
                on = remote(
                    B.at[sub], B.at[sub], b_send.at[kind, n, j], b_recv.at[kind, n, j],
                    up if kind == 0 else down,
                )
                last = rise == (7 if kind == 0 else 1)

                @pl.when(jnp.logical_not(is_source))
                def _():
                    on.wait_recv()

                @pl.when(jnp.logical_not(is_source | last))
                def _():
                    on.start()

        @pl.when(jnp.logical_not(at_origin))
        def _():
            for kind in range(2):
                at = (c,) + strip_of(kind, k, x, y)
                remote(B.at[at], B.at[at], e_send.at[kind, n, 0], e_recv.at[kind, n], sibling).start()

    def b_end(k):
        n = order[k]
        for kind in range(2):
            at = strip_of(kind, k, x, y)
            whole = (c,) + at
            swap = remote(B.at[whole], B.at[whole], e_send.at[kind, n, 0], e_recv.at[kind, n], sibling)
            last = rise == (7 if kind == 0 else 1)

            @pl.when(jnp.logical_not(is_source))
            def _():
                swap.wait_recv()

            @pl.when(jnp.logical_not(at_origin) | is_source)
            def _():
                swap.wait_send()

            for j in range(4):
                sub = (c,) + piece(kind, k, j)
                on = remote(
                    B.at[sub], B.at[sub], b_send.at[kind, n, j], b_recv.at[kind, n, j],
                    up if kind == 0 else down,
                )

                @pl.when(jnp.logical_not(last))
                def _():
                    on.wait_send()

                @pl.when(is_source)
                def _():
                    remote(
                        B.at[sub], B.at[sub], e_send.at[kind, n, 1 + j], b_recv.at[kind, n, j], sibling
                    ).wait_send()

            @pl.when(is_source)
            def _():
                for h in range(2):
                    pltpu.make_async_copy(
                        A.at[at + (pl.ds(512 * h, 512),)], B.at[(h,) + at], local_sem.at[kind, n, h]
                    ).wait()

    b_from_source(0)
    arrive(n_third)
    n_fourth = start(strips_on(half, 1))
    gifts += [give(kind, k) for k in (1, 3) for kind in range(2)]
    arrive(n_fourth)
    gifts += [give(kind, 2) for kind in range(2)]
    b_relay(0)
    arrive(a_third)
    a_fourth = start(strips_on(A, 0))
    b_from_source(1)
    b_from_source(3)
    arrive(a_fourth)
    b_from_source(2)
    for k in (1, 3, 2):
        b_relay(k)
    for copy in gifts:
        copy.wait()
    for k in (0, 1, 3, 2):
        b_end(k)
    for copies in (a_first, a_second, a_third, a_fourth, n_first, n_second, n_third, n_fourth):
        sent(copies)
    for copy in part_copies:
        copy.wait_send()
    for q in range(4):

        @pl.when(t == 0)
        def _():
            remote(
                A.at[x, y, chunks[q], pl.ds(512, 512)], N0.at[1, x, y, chunks[q]],
                sib_send.at[q], z_recv.at[q], sibling,
            ).wait_send()

        @pl.when(z < 4)
        def _():
            rising[q].wait_send()

        @pl.when((z == 0) | (z > 5))
        def _():
            falling[q].wait_send()


def gather(hidden, branch, gain, damping):
    vm = pl.BlockSpec(memory_space=pltpu.VMEM)
    dma = pltpu.SemaphoreType.DMA
    return pl.pallas_call(
        gather_body,
        out_shape=(
            jax.ShapeDtypeStruct((4, 4, 128, LEAD), bf16),
            jax.ShapeDtypeStruct((2, 4, 4, 128, LEAD // 2), bf16),
            jax.ShapeDtypeStruct((2, 4, 4, 128, LEAD // 2), bf16),
            jax.ShapeDtypeStruct((8, 128), f32),
        ),
        in_specs=[vm] * 4,
        out_specs=(vm,) * 4,
        scratch_shapes=[
            pltpu.VMEM((16, 16, 128), f32),
            dma((1,)),
            dma((16,)),
            dma((16,)),
            dma((2, 4)),
            dma((4,)),
            dma((4,)),
            dma((4,)),
            dma((2, 4, 2, 2)),
            dma((2, 4, 2, 2)),
            dma((2, 4)),
            dma((2, 4)),
            dma((2, 4, 4)),
            dma((2, 4, 4)),
            dma((2, 4, 5)),
            dma((2, 4)),
            dma((2, 4, 2)),
        ],
        compiler_params=pltpu.CompilerParams(
            collective_id=0, has_side_effects=True, vmem_limit_bytes=40 * 2**20
        ),
    )(hidden, branch, gain, damping)


def per_device(hidden, branch, gain, damping):
    gain, damping = gain.reshape(8, 128), damping.reshape(8, 128)
    A, B, N0, lead_damping = gather(hidden, branch, gain, damping)
    A = A.reshape(TOKENS, LEAD)
    B, N0 = B.reshape(2, TOKENS, LEAD // 2), N0.reshape(2, TOKENS, LEAD // 2)
    return compute(A, B, N0, lead_damping, damping)


def solution(mesh):
    return jax.shard_map(
        per_device,
        mesh=mesh,
        in_specs=(P("dp", "tensor"), P("dp", "tensor"), P("tensor"), P("tensor")),
        out_specs=(P("dp", "tensor"), P("dp", None), P("dp", None)),
        check_vma=False,
    )
```

```python
import functools

import jax
import jax.numpy as jnp
from jax import lax
from jax.experimental import pallas as pl
from jax.experimental.pallas import tpu as pltpu
from jax.sharding import PartitionSpec as P

D = 16384
TOKENS = 2048
LEAD = 1024
MESH = pl.DeviceIdType.MESH
f32, bf16 = jnp.float32, jnp.bfloat16
NN = (((1,), (0,)), ((), ()))
NT = (((1,), (1,)), ((), ()))
TN = (((0,), (0,)), ((), ()))


def split(x):
    high = x.astype(bf16)
    return high, (x - high.astype(f32)).astype(bf16)


def dot1(x, y, dims):
    return lax.dot_general(x, y, dims, preferred_element_type=f32)


def dot3(x, y, dims):
    (xh, xl), (yh, yl) = split(x), split(y)
    return dot1(xh, yh, dims) + (dot1(xh, yl, dims) + dot1(xl, yh, dims))


def iota(shape, dim):
    return lax.broadcasted_iota(jnp.int32, shape, dim)


def base_inverse(T, between=None, b=32, n=128):
    sub, lane = iota((b, n), 0), iota((b, n), 1)
    for o in range(0, n, b):
        if between is not None:
            between()
        R = T[o : o + b, :]
        C = [jnp.broadcast_to(R[:, o + j : o + j + 1], (b, n)) for j in range(b)]
        R = jnp.where((lane >= o) & (lane < o + b), (lane - o == sub).astype(f32), R)
        for j in range(b):
            r = lax.rsqrt(C[j][j : j + 1, :])
            column = jnp.where(sub > j, C[j] * r, 0.0)
            row = R[j : j + 1, :] * r
            R = jnp.where(sub == j, row, R - column * row)
            for m in range(j + 1, b):
                C[m] = C[m] - column * column[m : m + 1, :]
        T[o : o + b, :] = R
        lo = o + b
        if lo < n:
            (Uh, Ul), (Rh, Rl) = split(jnp.where(lane >= lo, R, 0.0)), split(R)
            update = dot1(
                jnp.concatenate([Uh, Uh, Ul], 0), jnp.concatenate([Rh, Rl, Rh], 0), TN
            )
            ln = iota((n - lo, n), 1)
            T[lo:, :] = jnp.where((ln >= o) & (ln < lo), 0.0, T[lo:, :]) - update[lo:, :]
    T[...] = jnp.where(iota((n, n), 0) >= iota((n, n), 1), T[...], 0.0)


def factor(T, block, between=None):
    n = LEAD // 128
    for k in range(n):
        rows = slice(k * 128, k * 128 + 128)
        block[...] = T[rows, rows]
        base_inverse(block, between)
        inverse = block[...]
        if k:
            T[rows, : k * 128] = dot3(inverse, T[rows, : k * 128], NN)
        T[rows, rows] = inverse
        if k < n - 1:
            right = slice(k * 128 + 128, LEAD)
            U = dot3(inverse, T[rows, right], NN)
            T[rows, right] = U
            Uh, Ul = split(U)
            left = T[rows, : k * 128 + 128]
            Lh, Ll = split(left)
            for i in range(k + 1, n):
                at = slice((i - k - 1) * 128, (i - k) * 128)
                own = slice(i * 128, i * 128 + 128)
                uh, ul = Uh[:, at].T, Ul[:, at].T
                low = dot1(uh, Lh, NN) + (dot1(uh, Ll, NN) + dot1(ul, Lh, NN))
                if k:
                    T[own, : k * 128] = T[own, : k * 128] - low[:, : k * 128]
                T[own, rows] = -low[:, k * 128 :]
                rest = slice((i - k - 1) * 128, None)
                T[own, i * 128 :] = T[own, i * 128 :] - (
                    dot1(uh, Uh[:, rest], NN)
                    + (dot1(uh, Ul[:, rest], NN) + dot1(ul, Uh[:, rest], NN))
                )


def compute_body(
    A, B, W, lead_t, lead_damping, own_damping, tile, first, second, rows_t, panel, moved_t
):
    dp, tensor = lax.axis_index("dp"), lax.axis_index("tensor")
    step = 256
    n = LEAD // step

    def turn(i, _):
        at = pl.ds(pl.multiple_of(i * 128, 128), 128)
        for h in range(2):
            rows_t[h * 512 : h * 512 + 512, at] = B[h, at, :].T
        return 0

    lax.fori_loop(0, TOKENS // 128, turn, 0)
    eye = iota((128, 128), 0) == iota((128, 128), 1)

    def gram_rows(i, _):
        at = pl.ds(pl.multiple_of(i * step, step), step)
        panel[at, :] = dot1(rows_t[at, :], lead_t[...], NT) * (1.0 / TOKENS)
        moved_t[at, :] = dot1(lead_t[at, :], A[...], NN) * (1.0 / TOKENS)
        tile[at, :] = dot1(rows_t[at, :], A[...], NN) * (1.0 / TOKENS)
        return 0

    lax.fori_loop(0, n, gram_rows, 0)

    def damp(ref, values):
        for k in range(LEAD // 128):
            at = slice(k * 128, k * 128 + 128)
            ref[at, at] = ref[at, at] + jnp.where(eye, values[k : k + 1, :], 0.0)

    @pl.when(dp == 0)
    def _():
        damp(panel, lead_damping)

    @pl.when(tensor == 0)
    def _():
        damp(moved_t, lead_damping)

    @pl.when(dp == tensor)
    def _():
        damp(tile, own_damping)

    for q in range(n - 1, -1, -1):
        own = slice(q * step, q * step + step)
        wide = (q + 1) * step
        wh, wl = split(W[own, :wide])
        sh, sl = split(panel[:, :wide])
        out = first if q < 2 else second
        out[:, (q % 2) * step : (q % 2) * step + step] = dot1(sh, wh, NT) + (
            dot1(sh, wl, NT) + dot1(sl, wh, NT)
        )
        sh, sl = split(moved_t[:wide, :])
        moved_t[own, :] = dot1(wh, sh, NN) + (dot1(wl, sh, NN) + dot1(wh, sl, NN))

    def finish(i, _):
        at = pl.ds(pl.multiple_of(i * step, step), step)
        left = jnp.concatenate([first[at, :], second[at, :]], 1)
        tile[at, :] = tile[at, :] - dot3(left, moved_t[...], NN)
        return 0

    lax.fori_loop(0, n, finish, 0)


def compute(A, B, W, lead_t, lead_damping, own_damping):
    vm = pl.BlockSpec(memory_space=pltpu.VMEM)
    return pl.pallas_call(
        compute_body,
        out_shape=(
            jax.ShapeDtypeStruct((LEAD, LEAD), f32),
            jax.ShapeDtypeStruct((LEAD, LEAD // 2), f32),
            jax.ShapeDtypeStruct((LEAD, LEAD // 2), f32),
        ),
        in_specs=[vm] * 6,
        out_specs=(vm,) * 3,
        scratch_shapes=[
            pltpu.VMEM((LEAD, TOKENS), bf16),
            pltpu.VMEM((LEAD, LEAD), f32),
            pltpu.VMEM((LEAD, LEAD), f32),
        ],
        compiler_params=pltpu.CompilerParams(vmem_limit_bytes=60 * 2**20),
    )(A, B, W, lead_t, lead_damping, own_damping)


def strip_of(kind, k, x, y):
    if kind == 0:
        return (slice(None), lax.rem(y + k, 4), pl.ds(0, 64))
    return (lax.rem(x + k, 4), slice(None), pl.ds(64, 64))


def gather_body(
    hidden, branch, gain, damping, A, B, T, lead_t, lead_damping,
    N0, block, parts, part_send, part_recv, z_send, z_recv, sib_send, sib_recv,
    g_send, g_recv, x_send, x_recv, b_send, b_recv, e_send, e_recv, local_sem,
):
    d, t = lax.axis_index("dp"), lax.axis_index("tensor")
    x, y, z, c = d // 4, d % 4, t // 2, t % 2
    sibling = (d, t + 1 - 2 * c)
    along = {
        (0, 1): (lax.rem(x + 1, 4) * 4 + y, t),
        (0, -1): (lax.rem(x + 3, 4) * 4 + y, t),
        (1, 1): (x * 4 + lax.rem(y + 1, 4), t),
        (1, -1): (x * 4 + lax.rem(y + 3, 4), t),
    }
    up = (d, lax.rem(z + 1, 8) * 2 + c)
    down = (d, lax.rem(z + 7, 8) * 2 + c)
    same = [(d, lax.rem(t + i, 16)) for i in range(1, 16)]

    everywhere = [(i, h) for i in range(8) for h in range(2)]
    takers = [(t, lax.rem(z + i, 8) * 2 + h) for i, h in everywhere]
    givers = [(lax.rem(d + i, 16), d) for i in range(16)]
    is_source = t == d

    barrier = pltpu.get_barrier_semaphore()

    def greet(partner):
        pl.semaphore_signal(barrier, inc=1, device_id=partner, device_id_type=MESH)

    for partner in same + list(along.values()):
        greet(partner)
    for partner in givers:
        greet(partner)

    def remote(src, dst, send, recv, to):
        return pltpu.make_async_remote_copy(
            src_ref=src, dst_ref=dst, send_sem=send, recv_sem=recv, device_id=to, device_id_type=MESH
        )

    total = hidden[...].astype(f32) + branch[...].astype(f32)
    own = jnp.broadcast_to(jnp.sum(total * total, axis=1, keepdims=True), (128, 128))
    parts[0, 0:8, :] = own.T[0:8, :]
    parts[0, 8:16, :] = damping[...]
    pl.semaphore_wait(barrier, 15 + 4 + 16)
    part_copies = [
        remote(parts.at[0], parts.at[i], part_send.at[i], part_recv.at[i], same[i - 1])
        for i in range(1, 16)
    ]
    for copy in part_copies:
        copy.start()
    for copy in part_copies:
        copy.wait_recv()
    squares = parts[0, 0:1, :]
    for i in range(1, 16):
        squares = squares + parts[i, 0:1, :]
    lead_damping[...] = parts[t, 8:16, :]
    scale = lax.rsqrt(squares / D + 1e-05)
    column = jnp.broadcast_to(scale, (128, 128)).T
    for j in range(8):
        at = slice(j * 128, j * 128 + 128)
        wide = hidden[:, at].astype(f32) + branch[:, at].astype(f32)
        A[x, y, :, at] = (wide * column * gain[j : j + 1, :]).astype(bf16)

    def both_ways(ref, which):
        copies = {}
        for kind in range(2):
            at = (x, y, pl.ds(64 * kind, 64))
            for side, s in ((1, 0), (-1, 1)):
                copies[kind, side] = remote(
                    ref.at[at], ref.at[at], g_send.at[which, 0, kind, s], g_recv.at[which, 0, kind, s],
                    along[kind, side],
                )
        return copies

    def pass_on(ref, which):
        copies = {}
        for kind in range(2):
            for side, s in ((1, 0), (-1, 1)):
                back = 4 - side
                at = (lax.rem(x + back, 4), y) if kind == 0 else (x, lax.rem(y + back, 4))
                at = at + (pl.ds(64 * kind + 32 * s, 32),)
                copies[kind, side] = remote(
                    ref.at[at], ref.at[at], g_send.at[which, 1, kind, s], g_recv.at[which, 1, kind, s],
                    along[kind, side],
                )
        return copies

    def strips(ref, which):
        copies = {}
        for kind in range(2):
            at = strip_of(kind, 0, x, y)
            for side, s in ((1, 0), (-1, 1)):
                copies[kind, side] = remote(
                    ref.at[at], ref.at[at], g_send.at[which, 2, kind, s], g_recv.at[which, 2, kind, s],
                    along[1 - kind, side],
                )
        return copies

    def strips_on(ref, which):
        copies = {}
        for kind in range(2):
            for side, s in ((1, 0), (-1, 1)):
                at = strip_of(kind, 4 - side, x, y)
                at = at[:2] + (pl.ds(64 * kind + 32 * s, 32),)
                copies[kind, side] = remote(
                    ref.at[at], ref.at[at], g_send.at[which, 3, kind, s], g_recv.at[which, 3, kind, s],
                    along[1 - kind, side],
                )
        return copies

    def start(copies):
        for copy in copies.values():
            copy.start()
        return copies

    def arrive(copies):
        for copy in copies.values():
            copy.wait_recv()

    def sent(copies):
        for copy in copies.values():
            copy.wait_send()

    a_first = start(both_ways(A, 0))

    half = N0.at[c]
    chunks = [pl.ds(32 * q, 32) for q in range(4)]
    source = (x, y)

    @pl.when(t == 0)
    def _():
        for q in range(4):
            remote(
                A.at[x, y, chunks[q], pl.ds(512, 512)], N0.at[1, x, y, chunks[q]],
                sib_send.at[q], z_recv.at[q], sibling,
            ).start()
        N0[0, x, y] = A[x, y, :, 0:512]

    rising, falling = [], []
    for q in range(4):
        at = half.at[source + (chunks[q],)]
        rising.append(remote(at, at, z_send.at[0, q], z_recv.at[q], up))
        falling.append(remote(at, at, z_send.at[1, q], z_recv.at[q], down))

        @pl.when(t != 0)
        def _():
            rising[q].wait_recv()

        @pl.when(z < 4)
        def _():
            rising[q].start()

        @pl.when((z == 0) | (z > 5))
        def _():
            falling[q].start()

    n_first = start(both_ways(half, 1))
    arrive(a_first)
    a_second = start(pass_on(A, 0))
    arrive(n_first)
    n_second = start(pass_on(half, 1))

    def give(kind, k):
        at = (c,) + strip_of(kind, k, x, y)
        copy = remote(N0.at[at], N0.at[at], x_send.at[kind, k], x_recv.at[kind, k], sibling)
        copy.start()
        return copy

    gifts = []
    arrive(n_second)
    n_third = start(strips(half, 1))
    gifts += [give(kind, 0) for kind in range(2)]
    arrive(a_second)
    a_third = start(strips(A, 0))

    def b_copy(i, h):
        to = takers[2 * i + h]
        src = A.at[x, y, :, pl.ds(512 * h, 512)]
        return remote(src, B.at[h, x, y], b_send.at[i, h], b_recv.at[d], to)

    def b_local(h):
        src = A.at[x, y, :, pl.ds(512 * h, 512)]
        return pltpu.make_async_copy(src, B.at[h, x, y], b_recv.at[d])

    def to_self(h):
        return is_source & (c == h)

    def b_start():
        for i, h in everywhere:
            if i:
                b_copy(i, h).start()
                continue

            @pl.when(jnp.logical_not(to_self(h)))
            def _():
                b_copy(i, h).start()

            @pl.when(to_self(h))
            def _():
                b_local(h).start()

    def b_swap(e):
        place = lax.rem(d + e, 16)
        at = B.at[c, place // 4, place % 4]
        remote(at, at, b_send.at[0, 0], b_recv.at[place], sibling).wait_recv()
        swap = remote(at, at, e_send.at[e], e_recv.at[e], sibling)
        swap.start()
        return swap

    arrive(n_third)
    n_fourth = start(strips_on(half, 1))
    gifts += [give(kind, k) for k in (1, 3) for kind in range(2)]
    arrive(n_fourth)
    gifts += [give(kind, 2) for kind in range(2)]
    b_start()
    arrive(a_third)
    a_fourth = start(strips_on(A, 0))
    for copy in gifts:
        copy.wait()

    def turn(i, _):
        at = pl.ds(pl.multiple_of(i * 128, 128), 128)
        for h in range(2):
            lead_t[h * 512 : h * 512 + 512, at] = N0[h, i // 4, i % 4].T
        return 0

    lax.fori_loop(0, 16, turn, 0)
    eye = iota((128, 128), 0) == iota((128, 128), 1)
    for k in range(LEAD // 128):
        rows = slice(k * 128, k * 128 + 128)
        for h in range(k // 4, 2):
            lo = k * 128 - h * 512 if h == k // 4 else 0
            right = N0[h].reshape(TOKENS, 512)[:, lo:]
            T[rows, h * 512 + lo : h * 512 + 512] = dot1(lead_t[rows, :], right, NN) * (1.0 / TOKENS)
        T[rows, rows] = T[rows, rows] + jnp.where(eye, lead_damping[k : k + 1, :], 0.0)
    swaps = []

    def between():
        calls[0] += 1
        if calls[0] % 2 == 0 and len(swaps) < 16:
            swaps.append(b_swap(len(swaps)))

    calls = [0]
    factor(T, block, between)
    for k in range(LEAD // 128 - 1):
        T[k * 128 : k * 128 + 128, k * 128 + 128 :] = jnp.zeros((128, LEAD - 128 - k * 128), f32)
    while len(swaps) < 16:
        swaps.append(b_swap(len(swaps)))
    arrive(a_fourth)
    for swap in swaps:
        swap.wait()
    for i, h in everywhere:
        if i:
            b_copy(i, h).wait_send()
            continue

        @pl.when(jnp.logical_not(to_self(h)))
        def _():
            b_copy(i, h).wait_send()

    for copies in (a_first, a_second, a_third, a_fourth, n_first, n_second, n_third, n_fourth):
        sent(copies)
    for copy in part_copies:
        copy.wait_send()
    for q in range(4):

        @pl.when(t == 0)
        def _():
            remote(
                A.at[x, y, chunks[q], pl.ds(512, 512)], N0.at[1, x, y, chunks[q]],
                sib_send.at[q], z_recv.at[q], sibling,
            ).wait_send()

        @pl.when(z < 4)
        def _():
            rising[q].wait_send()

        @pl.when((z == 0) | (z > 5))
        def _():
            falling[q].wait_send()


def gather(hidden, branch, gain, damping):
    vm = pl.BlockSpec(memory_space=pltpu.VMEM)
    dma = pltpu.SemaphoreType.DMA
    return pl.pallas_call(
        gather_body,
        out_shape=(
            jax.ShapeDtypeStruct((4, 4, 128, LEAD), bf16),
            jax.ShapeDtypeStruct((2, 4, 4, 128, LEAD // 2), bf16),
            jax.ShapeDtypeStruct((LEAD, LEAD), f32),
            jax.ShapeDtypeStruct((LEAD, TOKENS), bf16),
            jax.ShapeDtypeStruct((8, 128), f32),
        ),
        in_specs=[vm] * 4,
        out_specs=(vm,) * 5,
        scratch_shapes=[
            pltpu.VMEM((2, 4, 4, 128, LEAD // 2), bf16),
            pltpu.VMEM((128, 128), f32),
            pltpu.VMEM((16, 16, 128), f32),
            dma((16,)),
            dma((16,)),
            dma((2, 4)),
            dma((4,)),
            dma((4,)),
            dma((4,)),
            dma((2, 4, 2, 2)),
            dma((2, 4, 2, 2)),
            dma((2, 4)),
            dma((2, 4)),
            dma((8, 2)),
            dma((16,)),
            dma((16,)),
            dma((16,)),
            dma((1,)),
        ],
        compiler_params=pltpu.CompilerParams(
            collective_id=0, has_side_effects=True, vmem_limit_bytes=56 * 2**20
        ),
    )(hidden, branch, gain, damping)


def per_device(hidden, branch, gain, damping):
    gain, damping = gain.reshape(8, 128), damping.reshape(8, 128)
    A, B, W, lead_t, lead_damping = gather(hidden, branch, gain, damping)
    A = A.reshape(TOKENS, LEAD)
    B = B.reshape(2, TOKENS, LEAD // 2)
    return compute(A, B, W, lead_t, lead_damping, damping)


def solution(mesh):
    return jax.shard_map(
        per_device,
        mesh=mesh,
        in_specs=(P("dp", "tensor"), P("dp", "tensor"), P("tensor"), P("tensor")),
        out_specs=(P("dp", "tensor"), P("dp", None), P("dp", None)),
        check_vma=False,
    )
```

```python
import functools

import jax
import jax.numpy as jnp
from jax import lax
from jax.experimental import pallas as pl
from jax.experimental.pallas import tpu as pltpu
from jax.sharding import PartitionSpec as P

D = 16384
TOKENS = 2048
LEAD = 1024
MESH = pl.DeviceIdType.MESH
f32, bf16 = jnp.float32, jnp.bfloat16
NN = (((1,), (0,)), ((), ()))
NT = (((1,), (1,)), ((), ()))
TN = (((0,), (0,)), ((), ()))


def split(x):
    high = x.astype(bf16)
    return high, (x - high.astype(f32)).astype(bf16)


def dot1(x, y, dims):
    return lax.dot_general(x, y, dims, preferred_element_type=f32)


def dot3(x, y, dims):
    (xh, xl), (yh, yl) = split(x), split(y)
    return dot1(xh, yh, dims) + (dot1(xh, yl, dims) + dot1(xl, yh, dims))


def iota(shape, dim):
    return lax.broadcasted_iota(jnp.int32, shape, dim)


def base_inverse(T, between=None, b=32, n=128):
    sub, lane = iota((b, n), 0), iota((b, n), 1)
    for o in range(0, n, b):
        if between is not None:
            between()
        R = T[o : o + b, :]
        C = [jnp.broadcast_to(R[:, o + j : o + j + 1], (b, n)) for j in range(b)]
        R = jnp.where((lane >= o) & (lane < o + b), (lane - o == sub).astype(f32), R)
        for j in range(b):
            r = lax.rsqrt(C[j][j : j + 1, :])
            column = jnp.where(sub > j, C[j] * r, 0.0)
            row = R[j : j + 1, :] * r
            R = jnp.where(sub == j, row, R - column * row)
            for m in range(j + 1, b):
                C[m] = C[m] - column * column[m : m + 1, :]
        T[o : o + b, :] = R
        lo = o + b
        if lo < n:
            (Uh, Ul), (Rh, Rl) = split(jnp.where(lane >= lo, R, 0.0)), split(R)
            update = dot1(
                jnp.concatenate([Uh, Uh, Ul], 0), jnp.concatenate([Rh, Rl, Rh], 0), TN
            )
            ln = iota((n - lo, n), 1)
            T[lo:, :] = jnp.where((ln >= o) & (ln < lo), 0.0, T[lo:, :]) - update[lo:, :]
    T[...] = jnp.where(iota((n, n), 0) >= iota((n, n), 1), T[...], 0.0)


def factor(T, block, between=None):
    n = LEAD // 128
    for k in range(n):
        rows = slice(k * 128, k * 128 + 128)
        block[...] = T[rows, rows]
        base_inverse(block, between)
        inverse = block[...]
        if k:
            T[rows, : k * 128] = dot3(inverse, T[rows, : k * 128], NN)
        T[rows, rows] = inverse
        if k < n - 1:
            right = slice(k * 128 + 128, LEAD)
            U = dot3(inverse, T[rows, right], NN)
            T[rows, right] = U
            Uh, Ul = split(U)
            left = T[rows, : k * 128 + 128]
            Lh, Ll = split(left)
            for i in range(k + 1, n):
                at = slice((i - k - 1) * 128, (i - k) * 128)
                own = slice(i * 128, i * 128 + 128)
                uh, ul = Uh[:, at].T, Ul[:, at].T
                low = dot1(uh, Lh, NN) + (dot1(uh, Ll, NN) + dot1(ul, Lh, NN))
                if k:
                    T[own, : k * 128] = T[own, : k * 128] - low[:, : k * 128]
                T[own, rows] = -low[:, k * 128 :]
                rest = slice((i - k - 1) * 128, None)
                T[own, i * 128 :] = T[own, i * 128 :] - (
                    dot1(uh, Uh[:, rest], NN)
                    + (dot1(uh, Ul[:, rest], NN) + dot1(ul, Uh[:, rest], NN))
                )


def compute_body(
    A, B, W, lead_t, lead_damping, own_damping, tile, first, second, rows_t, panel, moved_t
):
    dp, tensor = lax.axis_index("dp"), lax.axis_index("tensor")
    step = 256
    n = LEAD // step

    def turn(i, _):
        at = pl.ds(pl.multiple_of(i * 128, 128), 128)
        for h in range(2):
            rows_t[h * 512 : h * 512 + 512, at] = B[h, at, :].T
        return 0

    lax.fori_loop(0, TOKENS // 128, turn, 0)
    eye = iota((128, 128), 0) == iota((128, 128), 1)

    def gram_rows(i, _):
        at = pl.ds(pl.multiple_of(i * step, step), step)
        panel[at, :] = dot1(rows_t[at, :], lead_t[...], NT) * (1.0 / TOKENS)
        moved_t[at, :] = dot1(lead_t[at, :], A[...], NN) * (1.0 / TOKENS)
        tile[at, :] = dot1(rows_t[at, :], A[...], NN) * (1.0 / TOKENS)
        return 0

    lax.fori_loop(0, n, gram_rows, 0)

    def damp(ref, values):
        for k in range(LEAD // 128):
            at = slice(k * 128, k * 128 + 128)
            ref[at, at] = ref[at, at] + jnp.where(eye, values[k : k + 1, :], 0.0)

    @pl.when(dp == 0)
    def _():
        damp(panel, lead_damping)

    @pl.when(tensor == 0)
    def _():
        damp(moved_t, lead_damping)

    @pl.when(dp == tensor)
    def _():
        damp(tile, own_damping)

    for q in range(n - 1, -1, -1):
        own = slice(q * step, q * step + step)
        wide = (q + 1) * step
        wh, wl = split(W[own, :wide])
        sh, sl = split(panel[:, :wide])
        out = first if q < 2 else second
        out[:, (q % 2) * step : (q % 2) * step + step] = dot1(sh, wh, NT) + (
            dot1(sh, wl, NT) + dot1(sl, wh, NT)
        )
        sh, sl = split(moved_t[:wide, :])
        moved_t[own, :] = dot1(wh, sh, NN) + (dot1(wl, sh, NN) + dot1(wh, sl, NN))

    def finish(i, _):
        at = pl.ds(pl.multiple_of(i * step, step), step)
        left = jnp.concatenate([first[at, :], second[at, :]], 1)
        tile[at, :] = tile[at, :] - dot3(left, moved_t[...], NN)
        return 0

    lax.fori_loop(0, n, finish, 0)


def compute(A, B, W, lead_t, lead_damping, own_damping):
    vm = pl.BlockSpec(memory_space=pltpu.VMEM)
    return pl.pallas_call(
        compute_body,
        out_shape=(
            jax.ShapeDtypeStruct((LEAD, LEAD), f32),
            jax.ShapeDtypeStruct((LEAD, LEAD // 2), f32),
            jax.ShapeDtypeStruct((LEAD, LEAD // 2), f32),
        ),
        in_specs=[vm] * 6,
        out_specs=(vm,) * 3,
        scratch_shapes=[
            pltpu.VMEM((LEAD, TOKENS), bf16),
            pltpu.VMEM((LEAD, LEAD), f32),
            pltpu.VMEM((LEAD, LEAD), f32),
        ],
        compiler_params=pltpu.CompilerParams(vmem_limit_bytes=60 * 2**20),
    )(A, B, W, lead_t, lead_damping, own_damping)


def strip_of(kind, k, x, y):
    if kind == 0:
        return (slice(None), lax.rem(y + k, 4), pl.ds(0, 64))
    return (lax.rem(x + k, 4), slice(None), pl.ds(64, 64))


def gather_body(
    hidden, branch, gain, damping, A, B, T, lead_t, lead_damping,
    N0, Z, block, parts, part_send, part_recv, z_send, z_recv, sib_send, sib_recv,
    g_send, g_recv, x_send, x_recv, b_send, b_recv, e_send, e_recv, ring_send, ring_recv,
):
    d, t = lax.axis_index("dp"), lax.axis_index("tensor")
    x, y, z, c = d // 4, d % 4, t // 2, t % 2
    sibling = (d, t + 1 - 2 * c)
    along = {
        (0, 1): (lax.rem(x + 1, 4) * 4 + y, t),
        (0, -1): (lax.rem(x + 3, 4) * 4 + y, t),
        (1, 1): (x * 4 + lax.rem(y + 1, 4), t),
        (1, -1): (x * 4 + lax.rem(y + 3, 4), t),
    }
    up = (d, lax.rem(z + 1, 8) * 2 + c)
    down = (d, lax.rem(z + 7, 8) * 2 + c)
    same = [(d, lax.rem(t + i, 16)) for i in range(1, 16)]

    plane = [(lax.rem(d + i, 16), t) for i in range(1, 16)]

    barrier = pltpu.get_barrier_semaphore()

    def greet(partner):
        pl.semaphore_signal(barrier, inc=1, device_id=partner, device_id_type=MESH)

    for partner in same + plane:
        greet(partner)

    def remote(src, dst, send, recv, to):
        return pltpu.make_async_remote_copy(
            src_ref=src, dst_ref=dst, send_sem=send, recv_sem=recv, device_id=to, device_id_type=MESH
        )

    total = hidden[...].astype(f32) + branch[...].astype(f32)
    own = jnp.broadcast_to(jnp.sum(total * total, axis=1, keepdims=True), (128, 128))
    parts[0, 0:8, :] = own.T[0:8, :]
    parts[0, 8:16, :] = damping[...]
    pl.semaphore_wait(barrier, 30)
    part_copies = [
        remote(parts.at[0], parts.at[i], part_send.at[i], part_recv.at[i], same[i - 1])
        for i in range(1, 16)
    ]
    for copy in part_copies:
        copy.start()
    for copy in part_copies:
        copy.wait_recv()
    squares = parts[0, 0:1, :]
    for i in range(1, 16):
        squares = squares + parts[i, 0:1, :]
    lead_damping[...] = parts[t, 8:16, :]
    scale = lax.rsqrt(squares / D + 1e-05)
    column = jnp.broadcast_to(scale, (128, 128)).T
    for j in range(8):
        at = slice(j * 128, j * 128 + 128)
        wide = hidden[:, at].astype(f32) + branch[:, at].astype(f32)
        A[x, y, :, at] = (wide * column * gain[j : j + 1, :]).astype(bf16)

    def both_ways(ref, which):
        copies = {}
        for kind in range(2):
            at = (x, y, pl.ds(64 * kind, 64))
            for side, s in ((1, 0), (-1, 1)):
                copies[kind, side] = remote(
                    ref.at[at], ref.at[at], g_send.at[which, 0, kind, s], g_recv.at[which, 0, kind, s],
                    along[kind, side],
                )
        return copies

    def pass_on(ref, which):
        copies = {}
        for kind in range(2):
            for side, s in ((1, 0), (-1, 1)):
                back = 4 - side
                at = (lax.rem(x + back, 4), y) if kind == 0 else (x, lax.rem(y + back, 4))
                at = at + (pl.ds(64 * kind + 32 * s, 32),)
                copies[kind, side] = remote(
                    ref.at[at], ref.at[at], g_send.at[which, 1, kind, s], g_recv.at[which, 1, kind, s],
                    along[kind, side],
                )
        return copies

    def strips(ref, which):
        copies = {}
        for kind in range(2):
            at = strip_of(kind, 0, x, y)
            for side, s in ((1, 0), (-1, 1)):
                copies[kind, side] = remote(
                    ref.at[at], ref.at[at], g_send.at[which, 2, kind, s], g_recv.at[which, 2, kind, s],
                    along[1 - kind, side],
                )
        return copies

    def strips_on(ref, which):
        copies = {}
        for kind in range(2):
            for side, s in ((1, 0), (-1, 1)):
                at = strip_of(kind, 4 - side, x, y)
                at = at[:2] + (pl.ds(64 * kind + 32 * s, 32),)
                copies[kind, side] = remote(
                    ref.at[at], ref.at[at], g_send.at[which, 3, kind, s], g_recv.at[which, 3, kind, s],
                    along[1 - kind, side],
                )
        return copies

    def start(copies):
        for copy in copies.values():
            copy.start()
        return copies

    def arrive(copies):
        for copy in copies.values():
            copy.wait_recv()

    def sent(copies):
        for copy in copies.values():
            copy.wait_send()

    half = N0.at[c]
    chunks = [pl.ds(32 * q, 32) for q in range(4)]
    source = (x, y)

    @pl.when(t == 0)
    def _():
        for q in range(4):
            remote(
                A.at[x, y, chunks[q], pl.ds(512, 512)], N0.at[1, x, y, chunks[q]],
                sib_send.at[q], z_recv.at[q], sibling,
            ).start()
        N0[0, x, y] = A[x, y, :, 0:512]

    mine = pl.ds(pl.multiple_of(c * 512, 512), 512)
    other = pl.ds(pl.multiple_of(512 - c * 512, 512), 512)
    pair_copy = remote(A.at[x, y, :, other], Z.at[t], ring_send.at[0, 0], ring_recv.at[0, 0], sibling)
    pair_copy.start()
    Z[t] = A[x, y, :, mine]
    a_first = start(both_ways(A, 0))

    def ring(s):
        below, above = lax.rem(z + 9 - s, 8) * 2, lax.rem(z + s - 1, 8) * 2
        if s < 4:
            parts_of = (pl.ds(below, 2), pl.ds(above, 2))
        else:
            parts_of = (pl.ds(below, 1), pl.ds(above + 1, 1))
        return {
            way: remote(
                Z.at[parts_of[way]], Z.at[parts_of[way]], ring_send.at[s, way], ring_recv.at[s, way], to
            )
            for way, to in ((0, up), (1, down))
        }

    rising, falling = [], []
    for q in range(4):
        at = half.at[source + (chunks[q],)]
        rising.append(remote(at, at, z_send.at[0, q], z_recv.at[q], up))
        falling.append(remote(at, at, z_send.at[1, q], z_recv.at[q], down))

        @pl.when(t != 0)
        def _():
            rising[q].wait_recv()

        @pl.when(z < 4)
        def _():
            rising[q].start()

        @pl.when((z == 0) | (z > 5))
        def _():
            falling[q].start()

    n_first = start(both_ways(half, 1))
    pair_copy.wait_recv()
    rings = [start(ring(1))]
    arrive(a_first)
    a_second = start(pass_on(A, 0))
    arrive(n_first)
    n_second = start(pass_on(half, 1))

    def give(kind, k):
        at = (c,) + strip_of(kind, k, x, y)
        copy = remote(N0.at[at], N0.at[at], x_send.at[kind, k], x_recv.at[kind, k], sibling)
        copy.start()
        return copy

    gifts = []
    arrive(n_second)
    n_third = start(strips(half, 1))
    gifts += [give(kind, 0) for kind in range(2)]
    arrive(rings[-1])
    rings.append(start(ring(2)))
    arrive(a_second)
    a_third = start(strips(A, 0))

    def b_copy(rel, b, begin):
        block_of = lax.rem(z + rel, 8) * 2 + b
        to = (block_of, t)
        at = B.at[c, x, y]

        @pl.when(block_of != d)
        def _():
            copy = remote(Z.at[block_of], at, b_send.at[rel, b], b_recv.at[d], to)
            if begin:
                copy.start()
            else:
                copy.wait_send()

        if begin:

            @pl.when(block_of == d)
            def _():
                pltpu.make_async_copy(Z.at[block_of], at, b_recv.at[d]).start()

    def b_swap(e):
        place = lax.rem(d + e, 16)
        at = B.at[c, place // 4, place % 4]
        remote(at, at, b_send.at[0, 0], b_recv.at[place], sibling).wait_recv()
        swap = remote(at, at, e_send.at[e], e_recv.at[e], sibling)
        swap.start()
        return swap

    arrive(n_third)
    n_fourth = start(strips_on(half, 1))
    gifts += [give(kind, k) for k in (1, 3) for kind in range(2)]
    arrive(rings[-1])
    rings.append(start(ring(3)))
    arrive(n_fourth)
    gifts += [give(kind, 2) for kind in range(2)]
    arrive(a_third)
    a_fourth = start(strips_on(A, 0))
    for rel in (0, 1, 7, 2, 6):
        for b in range(2):
            b_copy(rel, b, True)
    for copy in gifts:
        copy.wait()

    def turn(i, _):
        at = pl.ds(pl.multiple_of(i * 128, 128), 128)
        for h in range(2):
            lead_t[h * 512 : h * 512 + 512, at] = N0[h, i // 4, i % 4].T
        return 0

    lax.fori_loop(0, 16, turn, 0)
    eye = iota((128, 128), 0) == iota((128, 128), 1)
    for k in range(LEAD // 128):
        rows = slice(k * 128, k * 128 + 128)
        for h in range(k // 4, 2):
            lo = k * 128 - h * 512 if h == k // 4 else 0
            right = N0[h].reshape(TOKENS, 512)[:, lo:]
            T[rows, h * 512 + lo : h * 512 + 512] = dot1(lead_t[rows, :], right, NN) * (1.0 / TOKENS)
        T[rows, rows] = T[rows, rows] + jnp.where(eye, lead_damping[k : k + 1, :], 0.0)
    arrive(rings[-1])
    rings.append(start(ring(4)))
    for rel in (3, 5):
        for b in range(2):
            b_copy(rel, b, True)
    swaps = []

    def between():
        calls[0] += 1
        if calls[0] == 8:
            arrive(rings[-1])
            for b in range(2):
                b_copy(4, b, True)
        if calls[0] >= 17:
            swaps.append(b_swap(len(swaps)))

    calls = [0]
    factor(T, block, between)
    for k in range(LEAD // 128 - 1):
        T[k * 128 : k * 128 + 128, k * 128 + 128 :] = jnp.zeros((128, LEAD - 128 - k * 128), f32)
    while len(swaps) < 16:
        swaps.append(b_swap(len(swaps)))
    arrive(a_fourth)
    for swap in swaps:
        swap.wait()
    for rel in range(8):
        for b in range(2):
            b_copy(rel, b, False)
    for copies in rings:
        sent(copies)
    pair_copy.wait_send()
    for copies in (a_first, a_second, a_third, a_fourth, n_first, n_second, n_third, n_fourth):
        sent(copies)
    for copy in part_copies:
        copy.wait_send()
    for q in range(4):

        @pl.when(t == 0)
        def _():
            remote(
                A.at[x, y, chunks[q], pl.ds(512, 512)], N0.at[1, x, y, chunks[q]],
                sib_send.at[q], z_recv.at[q], sibling,
            ).wait_send()

        @pl.when(z < 4)
        def _():
            rising[q].wait_send()

        @pl.when((z == 0) | (z > 5))
        def _():
            falling[q].wait_send()


def gather(hidden, branch, gain, damping):
    vm = pl.BlockSpec(memory_space=pltpu.VMEM)
    dma = pltpu.SemaphoreType.DMA
    return pl.pallas_call(
        gather_body,
        out_shape=(
            jax.ShapeDtypeStruct((4, 4, 128, LEAD), bf16),
            jax.ShapeDtypeStruct((2, 4, 4, 128, LEAD // 2), bf16),
            jax.ShapeDtypeStruct((LEAD, LEAD), f32),
            jax.ShapeDtypeStruct((LEAD, TOKENS), bf16),
            jax.ShapeDtypeStruct((8, 128), f32),
        ),
        in_specs=[vm] * 4,
        out_specs=(vm,) * 5,
        scratch_shapes=[
            pltpu.VMEM((2, 4, 4, 128, LEAD // 2), bf16),
            pltpu.VMEM((16, 128, LEAD // 2), bf16),
            pltpu.VMEM((128, 128), f32),
            pltpu.VMEM((16, 16, 128), f32),
            dma((16,)),
            dma((16,)),
            dma((2, 4)),
            dma((4,)),
            dma((4,)),
            dma((4,)),
            dma((2, 4, 2, 2)),
            dma((2, 4, 2, 2)),
            dma((2, 4)),
            dma((2, 4)),
            dma((8, 2)),
            dma((16,)),
            dma((16,)),
            dma((16,)),
            dma((5, 2)),
            dma((5, 2)),
        ],
        compiler_params=pltpu.CompilerParams(
            collective_id=0, has_side_effects=True, vmem_limit_bytes=56 * 2**20
        ),
    )(hidden, branch, gain, damping)


def per_device(hidden, branch, gain, damping):
    gain, damping = gain.reshape(8, 128), damping.reshape(8, 128)
    A, B, W, lead_t, lead_damping = gather(hidden, branch, gain, damping)
    A = A.reshape(TOKENS, LEAD)
    B = B.reshape(2, TOKENS, LEAD // 2)
    return compute(A, B, W, lead_t, lead_damping, damping)


def solution(mesh):
    return jax.shard_map(
        per_device,
        mesh=mesh,
        in_specs=(P("dp", "tensor"), P("dp", "tensor"), P("tensor"), P("tensor")),
        out_specs=(P("dp", "tensor"), P("dp", None), P("dp", None)),
        check_vma=False,
    )
```

```python
import functools

import jax
import jax.numpy as jnp
from jax import lax
from jax.experimental import pallas as pl
from jax.experimental.pallas import tpu as pltpu
from jax.sharding import PartitionSpec as P

D = 16384
TOKENS = 2048
LEAD = 1024
MESH = pl.DeviceIdType.MESH
f32, bf16 = jnp.float32, jnp.bfloat16
NN = (((1,), (0,)), ((), ()))
NT = (((1,), (1,)), ((), ()))
TN = (((0,), (0,)), ((), ()))


def split(x):
    high = x.astype(bf16)
    return high, (x - high.astype(f32)).astype(bf16)


def dot1(x, y, dims):
    return lax.dot_general(x, y, dims, preferred_element_type=f32)


def dot3(x, y, dims):
    (xh, xl), (yh, yl) = split(x), split(y)
    return dot1(xh, yh, dims) + (dot1(xh, yl, dims) + dot1(xl, yh, dims))


def iota(shape, dim):
    return lax.broadcasted_iota(jnp.int32, shape, dim)


def base_inverse(T, between=None, b=32, n=128):
    sub, lane = iota((b, n), 0), iota((b, n), 1)
    for o in range(0, n, b):
        if between is not None:
            between()
        R = T[o : o + b, :]
        C = [jnp.broadcast_to(R[:, o + j : o + j + 1], (b, n)) for j in range(b)]
        R = jnp.where((lane >= o) & (lane < o + b), (lane - o == sub).astype(f32), R)
        for j in range(b):
            r = lax.rsqrt(C[j][j : j + 1, :])
            column = jnp.where(sub > j, C[j] * r, 0.0)
            row = R[j : j + 1, :] * r
            R = jnp.where(sub == j, row, R - column * row)
            for m in range(j + 1, b):
                C[m] = C[m] - column * column[m : m + 1, :]
        T[o : o + b, :] = R
        lo = o + b
        if lo < n:
            (Uh, Ul), (Rh, Rl) = split(jnp.where(lane >= lo, R, 0.0)), split(R)
            update = dot1(
                jnp.concatenate([Uh, Uh, Ul], 0), jnp.concatenate([Rh, Rl, Rh], 0), TN
            )
            ln = iota((n - lo, n), 1)
            T[lo:, :] = jnp.where((ln >= o) & (ln < lo), 0.0, T[lo:, :]) - update[lo:, :]
    T[...] = jnp.where(iota((n, n), 0) >= iota((n, n), 1), T[...], 0.0)


def factor(T, block, between=None, final=None):
    n = LEAD // 128
    for k in range(n):
        rows = slice(k * 128, k * 128 + 128)
        block[...] = T[rows, rows]
        base_inverse(block, between)
        inverse = block[...]
        if k:
            T[rows, : k * 128] = dot3(inverse, T[rows, : k * 128], NN)
        T[rows, rows] = inverse
        if k < n - 1:
            right = slice(k * 128 + 128, LEAD)
            U = dot3(inverse, T[rows, right], NN)
            T[rows, right] = U
            Uh, Ul = split(U)
            left = T[rows, : k * 128 + 128]
            Lh, Ll = split(left)
            for i in range(k + 1, n):
                at = slice((i - k - 1) * 128, (i - k) * 128)
                own = slice(i * 128, i * 128 + 128)
                uh, ul = Uh[:, at].T, Ul[:, at].T
                low = dot1(uh, Lh, NN) + (dot1(uh, Ll, NN) + dot1(ul, Lh, NN))
                if k:
                    T[own, : k * 128] = T[own, : k * 128] - low[:, : k * 128]
                T[own, rows] = -low[:, k * 128 :]
                rest = slice((i - k - 1) * 128, None)
                T[own, i * 128 :] = T[own, i * 128 :] - (
                    dot1(uh, Uh[:, rest], NN)
                    + (dot1(uh, Ul[:, rest], NN) + dot1(ul, Uh[:, rest], NN))
                )
        if final is not None:
            final(k)


def compute_body(
    A_in, B_in, W_in, lead_in, lead_damping, own_damping, tile_out, first_out, second_out,
    A, B, W, lead_t, tile, first, second, rows_t, panel, moved_t, in_sem, out_sem,
):
    dp, tensor = lax.axis_index("dp"), lax.axis_index("tensor")
    step = 256
    n = LEAD // step
    ins = [
        pltpu.make_async_copy(src, dst, in_sem.at[i])
        for i, (src, dst) in enumerate(((B_in, B), (lead_in, lead_t), (A_in, A), (W_in, W)))
    ]
    for copy in ins:
        copy.start()
    ins[0].wait()

    def turn(i, _):
        at = pl.ds(pl.multiple_of(i * 128, 128), 128)
        for h in range(2):
            rows_t[h * 512 : h * 512 + 512, at] = B[h, at, :].T
        return 0

    lax.fori_loop(0, TOKENS // 128, turn, 0)
    eye = iota((128, 128), 0) == iota((128, 128), 1)

    ins[1].wait()
    ins[2].wait()

    def gram_rows(i, _):
        at = pl.ds(pl.multiple_of(i * step, step), step)
        panel[at, :] = dot1(rows_t[at, :], lead_t[...], NT) * (1.0 / TOKENS)
        moved_t[at, :] = dot1(lead_t[at, :], A[...], NN) * (1.0 / TOKENS)
        tile[at, :] = dot1(rows_t[at, :], A[...], NN) * (1.0 / TOKENS)
        return 0

    lax.fori_loop(0, n, gram_rows, 0)

    def damp(ref, values):
        for k in range(LEAD // 128):
            at = slice(k * 128, k * 128 + 128)
            ref[at, at] = ref[at, at] + jnp.where(eye, values[k : k + 1, :], 0.0)

    @pl.when(dp == 0)
    def _():
        damp(panel, lead_damping)

    @pl.when(tensor == 0)
    def _():
        damp(moved_t, lead_damping)

    @pl.when(dp == tensor)
    def _():
        damp(tile, own_damping)

    ins[3].wait()
    for q in range(n - 1, -1, -1):
        own = slice(q * step, q * step + step)
        wide = (q + 1) * step
        wh, wl = split(W[own, :wide])
        sh, sl = split(panel[:, :wide])
        out = first if q < 2 else second
        out[:, (q % 2) * step : (q % 2) * step + step] = dot1(sh, wh, NT) + (
            dot1(sh, wl, NT) + dot1(sl, wh, NT)
        )
        sh, sl = split(moved_t[:wide, :])
        moved_t[own, :] = dot1(wh, sh, NN) + (dot1(wl, sh, NN) + dot1(wh, sl, NN))

    outs = [
        pltpu.make_async_copy(first, first_out, out_sem.at[n]),
        pltpu.make_async_copy(second, second_out, out_sem.at[n + 1]),
    ]
    for copy in outs:
        copy.start()

    def strip(i):
        at = pl.ds(pl.multiple_of(i * step, step), step)
        return pltpu.make_async_copy(tile.at[at], tile_out.at[at], out_sem.at[i])

    def finish(i, _):
        at = pl.ds(pl.multiple_of(i * step, step), step)
        left = jnp.concatenate([first[at, :], second[at, :]], 1)
        tile[at, :] = tile[at, :] - dot3(left, moved_t[...], NN)
        strip(i).start()
        return 0

    lax.fori_loop(0, n, finish, 0)
    for i in range(n):
        strip(i).wait()
    for copy in outs:
        copy.wait()


def compute(A, B, W, lead_t, lead_damping, own_damping):
    vm = pl.BlockSpec(memory_space=pltpu.VMEM)
    hbm = pl.BlockSpec(memory_space=pl.ANY)
    return pl.pallas_call(
        compute_body,
        out_shape=(
            jax.ShapeDtypeStruct((LEAD, LEAD), f32),
            jax.ShapeDtypeStruct((LEAD, LEAD // 2), f32),
            jax.ShapeDtypeStruct((LEAD, LEAD // 2), f32),
        ),
        in_specs=[hbm] * 4 + [vm] * 2,
        out_specs=(hbm,) * 3,
        scratch_shapes=[
            pltpu.VMEM((TOKENS, LEAD), bf16),
            pltpu.VMEM((2, TOKENS, LEAD // 2), bf16),
            pltpu.VMEM((LEAD, LEAD), f32),
            pltpu.VMEM((LEAD, TOKENS), bf16),
            pltpu.VMEM((LEAD, LEAD), f32),
            pltpu.VMEM((LEAD, LEAD // 2), f32),
            pltpu.VMEM((LEAD, LEAD // 2), f32),
            pltpu.VMEM((LEAD, TOKENS), bf16),
            pltpu.VMEM((LEAD, LEAD), f32),
            pltpu.VMEM((LEAD, LEAD), f32),
            pltpu.SemaphoreType.DMA((4,)),
            pltpu.SemaphoreType.DMA((6,)),
        ],
        compiler_params=pltpu.CompilerParams(vmem_limit_bytes=60 * 2**20),
    )(A, B, W, lead_t, lead_damping, own_damping)


def strip_of(kind, k, x, y):
    if kind == 0:
        return (slice(None), lax.rem(y + k, 4), pl.ds(0, 64))
    return (lax.rem(x + k, 4), slice(None), pl.ds(64, 64))


def gather_body(
    hidden, branch, gain, damping, A_out, B_out, T_out, lead_out, lead_damping,
    A, B, T, lead_t, out_sem, N0, Z, block, parts, part_send, part_recv, z_send, z_recv, sib_send, sib_recv,
    g_send, g_recv, x_send, x_recv, b_send, b_recv, e_send, e_recv, ring_send, ring_recv,
):
    d, t = lax.axis_index("dp"), lax.axis_index("tensor")
    x, y, z, c = d // 4, d % 4, t // 2, t % 2
    sibling = (d, t + 1 - 2 * c)
    along = {
        (0, 1): (lax.rem(x + 1, 4) * 4 + y, t),
        (0, -1): (lax.rem(x + 3, 4) * 4 + y, t),
        (1, 1): (x * 4 + lax.rem(y + 1, 4), t),
        (1, -1): (x * 4 + lax.rem(y + 3, 4), t),
    }
    up = (d, lax.rem(z + 1, 8) * 2 + c)
    down = (d, lax.rem(z + 7, 8) * 2 + c)
    same = [(d, lax.rem(t + i, 16)) for i in range(1, 16)]

    plane = [(lax.rem(d + i, 16), t) for i in range(1, 16)]

    barrier = pltpu.get_barrier_semaphore()

    def greet(partner):
        pl.semaphore_signal(barrier, inc=1, device_id=partner, device_id_type=MESH)

    for partner in same + plane:
        greet(partner)

    def remote(src, dst, send, recv, to):
        return pltpu.make_async_remote_copy(
            src_ref=src, dst_ref=dst, send_sem=send, recv_sem=recv, device_id=to, device_id_type=MESH
        )

    total = hidden[...].astype(f32) + branch[...].astype(f32)
    own = jnp.broadcast_to(jnp.sum(total * total, axis=1, keepdims=True), (128, 128))
    parts[0, 0:8, :] = own.T[0:8, :]
    parts[0, 8:16, :] = damping[...]
    pl.semaphore_wait(barrier, 30)
    part_copies = [
        remote(parts.at[0], parts.at[i], part_send.at[i], part_recv.at[i], same[i - 1])
        for i in range(1, 16)
    ]
    for copy in part_copies:
        copy.start()
    for copy in part_copies:
        copy.wait_recv()
    squares = parts[0, 0:1, :]
    for i in range(1, 16):
        squares = squares + parts[i, 0:1, :]
    lead_damping[...] = parts[t, 8:16, :]
    scale = lax.rsqrt(squares / D + 1e-05)
    column = jnp.broadcast_to(scale, (128, 128)).T
    for j in range(8):
        at = slice(j * 128, j * 128 + 128)
        wide = hidden[:, at].astype(f32) + branch[:, at].astype(f32)
        A[x, y, :, at] = (wide * column * gain[j : j + 1, :]).astype(bf16)

    def both_ways(ref, which):
        copies = {}
        for kind in range(2):
            at = (x, y, pl.ds(64 * kind, 64))
            for side, s in ((1, 0), (-1, 1)):
                copies[kind, side] = remote(
                    ref.at[at], ref.at[at], g_send.at[which, 0, kind, s], g_recv.at[which, 0, kind, s],
                    along[kind, side],
                )
        return copies

    def pass_on(ref, which):
        copies = {}
        for kind in range(2):
            for side, s in ((1, 0), (-1, 1)):
                back = 4 - side
                at = (lax.rem(x + back, 4), y) if kind == 0 else (x, lax.rem(y + back, 4))
                at = at + (pl.ds(64 * kind + 32 * s, 32),)
                copies[kind, side] = remote(
                    ref.at[at], ref.at[at], g_send.at[which, 1, kind, s], g_recv.at[which, 1, kind, s],
                    along[kind, side],
                )
        return copies

    def strips(ref, which):
        copies = {}
        for kind in range(2):
            at = strip_of(kind, 0, x, y)
            for side, s in ((1, 0), (-1, 1)):
                copies[kind, side] = remote(
                    ref.at[at], ref.at[at], g_send.at[which, 2, kind, s], g_recv.at[which, 2, kind, s],
                    along[1 - kind, side],
                )
        return copies

    def strips_on(ref, which):
        copies = {}
        for kind in range(2):
            for side, s in ((1, 0), (-1, 1)):
                at = strip_of(kind, 4 - side, x, y)
                at = at[:2] + (pl.ds(64 * kind + 32 * s, 32),)
                copies[kind, side] = remote(
                    ref.at[at], ref.at[at], g_send.at[which, 3, kind, s], g_recv.at[which, 3, kind, s],
                    along[1 - kind, side],
                )
        return copies

    def start(copies):
        for copy in copies.values():
            copy.start()
        return copies

    def arrive(copies):
        for copy in copies.values():
            copy.wait_recv()

    def sent(copies):
        for copy in copies.values():
            copy.wait_send()

    half = N0.at[c]
    chunks = [pl.ds(32 * q, 32) for q in range(4)]
    source = (x, y)

    @pl.when(t == 0)
    def _():
        for q in range(4):
            remote(
                A.at[x, y, chunks[q], pl.ds(512, 512)], N0.at[1, x, y, chunks[q]],
                sib_send.at[q], z_recv.at[q], sibling,
            ).start()
        N0[0, x, y] = A[x, y, :, 0:512]

    mine = pl.ds(pl.multiple_of(c * 512, 512), 512)
    other = pl.ds(pl.multiple_of(512 - c * 512, 512), 512)
    pair_copy = remote(A.at[x, y, :, other], Z.at[t], ring_send.at[0, 0], ring_recv.at[0, 0], sibling)
    pair_copy.start()
    Z[t] = A[x, y, :, mine]
    a_first = start(both_ways(A, 0))

    def ring(s):
        below, above = lax.rem(z + 9 - s, 8) * 2, lax.rem(z + s - 1, 8) * 2
        if s < 4:
            parts_of = (pl.ds(below, 2), pl.ds(above, 2))
        else:
            parts_of = (pl.ds(below, 1), pl.ds(above + 1, 1))
        return {
            way: remote(
                Z.at[parts_of[way]], Z.at[parts_of[way]], ring_send.at[s, way], ring_recv.at[s, way], to
            )
            for way, to in ((0, up), (1, down))
        }

    rising, falling = [], []
    for q in range(4):
        at = half.at[source + (chunks[q],)]
        rising.append(remote(at, at, z_send.at[0, q], z_recv.at[q], up))
        falling.append(remote(at, at, z_send.at[1, q], z_recv.at[q], down))

        @pl.when(t != 0)
        def _():
            rising[q].wait_recv()

        @pl.when(z < 4)
        def _():
            rising[q].start()

        @pl.when((z == 0) | (z > 5))
        def _():
            falling[q].start()

    n_first = start(both_ways(half, 1))
    pair_copy.wait_recv()
    rings = [start(ring(1))]
    arrive(a_first)
    a_second = start(pass_on(A, 0))
    arrive(n_first)
    n_second = start(pass_on(half, 1))

    def give(kind, k):
        at = (c,) + strip_of(kind, k, x, y)
        copy = remote(N0.at[at], N0.at[at], x_send.at[kind, k], x_recv.at[kind, k], sibling)
        copy.start()
        return copy

    gifts = []
    arrive(n_second)
    n_third = start(strips(half, 1))
    gifts += [give(kind, 0) for kind in range(2)]
    arrive(rings[-1])
    rings.append(start(ring(2)))
    arrive(a_second)
    a_third = start(strips(A, 0))

    def b_copy(rel, b, begin):
        block_of = lax.rem(z + rel, 8) * 2 + b
        to = (block_of, t)
        at = B.at[c, x, y]

        @pl.when(block_of != d)
        def _():
            copy = remote(Z.at[block_of], at, b_send.at[rel, b], b_recv.at[d], to)
            if begin:
                copy.start()
            else:
                copy.wait_send()

        if begin:

            @pl.when(block_of == d)
            def _():
                pltpu.make_async_copy(Z.at[block_of], at, b_recv.at[d]).start()

    def b_swap(e):
        place = lax.rem(d + e, 16)
        at = B.at[c, place // 4, place % 4]
        remote(at, at, b_send.at[0, 0], b_recv.at[place], sibling).wait_recv()
        swap = remote(at, at, e_send.at[e], e_recv.at[e], sibling)
        swap.start()
        return swap

    arrive(n_third)
    n_fourth = start(strips_on(half, 1))
    gifts += [give(kind, k) for k in (1, 3) for kind in range(2)]
    arrive(rings[-1])
    rings.append(start(ring(3)))
    arrive(n_fourth)
    gifts += [give(kind, 2) for kind in range(2)]
    arrive(a_third)
    a_fourth = start(strips_on(A, 0))
    for rel in (0, 1, 7, 2, 6):
        for b in range(2):
            b_copy(rel, b, True)
    for copy in gifts:
        copy.wait()

    def turn(i, _):
        at = pl.ds(pl.multiple_of(i * 128, 128), 128)
        for h in range(2):
            lead_t[h * 512 : h * 512 + 512, at] = N0[h, i // 4, i % 4].T
        return 0

    lax.fori_loop(0, 16, turn, 0)
    outs = [pltpu.make_async_copy(lead_t, lead_out, out_sem.at[0])]
    outs[0].start()
    eye = iota((128, 128), 0) == iota((128, 128), 1)
    for k in range(LEAD // 128):
        rows = slice(k * 128, k * 128 + 128)
        for h in range(k // 4, 2):
            lo = k * 128 - h * 512 if h == k // 4 else 0
            right = N0[h].reshape(TOKENS, 512)[:, lo:]
            T[rows, h * 512 + lo : h * 512 + 512] = dot1(lead_t[rows, :], right, NN) * (1.0 / TOKENS)
        T[rows, rows] = T[rows, rows] + jnp.where(eye, lead_damping[k : k + 1, :], 0.0)
    arrive(rings[-1])
    rings.append(start(ring(4)))
    for rel in (3, 5):
        for b in range(2):
            b_copy(rel, b, True)
    swaps = []

    def between():
        calls[0] += 1
        if calls[0] == 8:
            arrive(rings[-1])
            for b in range(2):
                b_copy(4, b, True)
        if calls[0] == 14:
            arrive(a_fourth)
            outs.append(pltpu.make_async_copy(A, A_out, out_sem.at[1]))
            outs[-1].start()
        if calls[0] >= 17:
            swaps.append(b_swap(len(swaps)))

    calls = [0]

    def final(k):
        rows = slice(k * 128, k * 128 + 128)
        if k < LEAD // 128 - 1:
            T[rows, k * 128 + 128 :] = jnp.zeros((128, LEAD - 128 - k * 128), f32)
        outs.append(
            pltpu.make_async_copy(T.at[pl.ds(k * 128, 128)], T_out.at[pl.ds(k * 128, 128)], out_sem.at[3 + k])
        )
        outs[-1].start()

    factor(T, block, between, final)
    while len(swaps) < 16:
        swaps.append(b_swap(len(swaps)))
    for swap in swaps:
        swap.wait()
    outs.append(pltpu.make_async_copy(B, B_out, out_sem.at[2]))
    outs[-1].start()
    for rel in range(8):
        for b in range(2):
            b_copy(rel, b, False)
    for copies in rings:
        sent(copies)
    pair_copy.wait_send()
    for copy in outs:
        copy.wait()
    for copies in (a_first, a_second, a_third, a_fourth, n_first, n_second, n_third, n_fourth):
        sent(copies)
    for copy in part_copies:
        copy.wait_send()
    for q in range(4):

        @pl.when(t == 0)
        def _():
            remote(
                A.at[x, y, chunks[q], pl.ds(512, 512)], N0.at[1, x, y, chunks[q]],
                sib_send.at[q], z_recv.at[q], sibling,
            ).wait_send()

        @pl.when(z < 4)
        def _():
            rising[q].wait_send()

        @pl.when((z == 0) | (z > 5))
        def _():
            falling[q].wait_send()


def gather(hidden, branch, gain, damping):
    vm = pl.BlockSpec(memory_space=pltpu.VMEM)
    dma = pltpu.SemaphoreType.DMA
    return pl.pallas_call(
        gather_body,
        out_shape=(
            jax.ShapeDtypeStruct((4, 4, 128, LEAD), bf16),
            jax.ShapeDtypeStruct((2, 4, 4, 128, LEAD // 2), bf16),
            jax.ShapeDtypeStruct((LEAD, LEAD), f32),
            jax.ShapeDtypeStruct((LEAD, TOKENS), bf16),
            jax.ShapeDtypeStruct((8, 128), f32),
        ),
        in_specs=[vm] * 4,
        out_specs=(pl.BlockSpec(memory_space=pl.ANY),) * 4 + (vm,),
        scratch_shapes=[
            pltpu.VMEM((4, 4, 128, LEAD), bf16),
            pltpu.VMEM((2, 4, 4, 128, LEAD // 2), bf16),
            pltpu.VMEM((LEAD, LEAD), f32),
            pltpu.VMEM((LEAD, TOKENS), bf16),
            dma((11,)),
            pltpu.VMEM((2, 4, 4, 128, LEAD // 2), bf16),
            pltpu.VMEM((16, 128, LEAD // 2), bf16),
            pltpu.VMEM((128, 128), f32),
            pltpu.VMEM((16, 16, 128), f32),
            dma((16,)),
            dma((16,)),
            dma((2, 4)),
            dma((4,)),
            dma((4,)),
            dma((4,)),
            dma((2, 4, 2, 2)),
            dma((2, 4, 2, 2)),
            dma((2, 4)),
            dma((2, 4)),
            dma((8, 2)),
            dma((16,)),
            dma((16,)),
            dma((16,)),
            dma((5, 2)),
            dma((5, 2)),
        ],
        compiler_params=pltpu.CompilerParams(
            collective_id=0, has_side_effects=True, vmem_limit_bytes=56 * 2**20
        ),
    )(hidden, branch, gain, damping)


def per_device(hidden, branch, gain, damping):
    gain, damping = gain.reshape(8, 128), damping.reshape(8, 128)
    A, B, W, lead_t, lead_damping = gather(hidden, branch, gain, damping)
    A = A.reshape(TOKENS, LEAD)
    B = B.reshape(2, TOKENS, LEAD // 2)
    return compute(A, B, W, lead_t, lead_damping, damping)


def solution(mesh):
    return jax.shard_map(
        per_device,
        mesh=mesh,
        in_specs=(P("dp", "tensor"), P("dp", "tensor"), P("tensor"), P("tensor")),
        out_specs=(P("dp", "tensor"), P("dp", None), P("dp", None)),
        check_vma=False,
    )
```
